32 devices in a mesh: rep: 2 (over y), slab: 4 (over x, core), head: 4 (over z).
Axes of the slice: x: 2, y: 2, z: 4, core: 2. Of those that a mesh axis runs over, the one named last changes fastest.
Arguments:
- atom_feats: bfloat16 [32768, 512], P(('rep', 'slab', 'head')), parts along dimension 0, may hold values from -56 to 56
- w_qkv: bfloat16 [512, 16, 96], replicated, may hold values from -0.5 to 0.5
- w_out: bfloat16 [512, 512], replicated, may hold values from -0.25 to 0.25
- neighbours: int32 [256, 8], P(('rep', 'slab')), parts along dimension 0, may hold values from 0 to 127, as said below
- counts: int32 [256], P('rep'), parts along dimension 0, may hold values from 32 to 128, as said below
- d_out: bfloat16 [32768, 512], P(('rep', 'slab', 'head')), parts along dimension 0, may hold values from -6 to 6
Outputs:
- layer_out: bfloat16 [32768, 512], P(('rep', 'slab', 'head')), parts along dimension 0
- grad_x: bfloat16 [32768, 512], P(('rep', 'slab', 'head')), parts along dimension 0
- grad_wo: float32 [1024, 512], P(('rep', 'head'), 'slab'), parts along dimension 0
The draws below stay inside these ranges and needn't reach their ends.
There are 2 independent parts, one for each index of `rep`. The reference program is written for one: setup_inputs(seed, part) draws one part's arguments, and reference() takes and returns one part's arrays. A program takes and returns all parts, laid end to end along the dimension named above; an argument that names none is the same for every part. Nothing has to cross between parts.
Inputs may be any that keep to these rules, and one draw needn't show every extreme that they name: `neighbours`: row b lists 8 different blocks, b itself first; every other listed block lies at most 16 positions from b in the cyclic order of the 128 blocks, and the last entry lies exactly 16 positions away. `counts`: in every aligned group of four blocks one block holds 128 atoms and another 128 // 4.
All inputs are finite; a program needn't handle non-finite values.
Results may differ from the reference program's by a relative error of at most 0.014.
The reference program's roundings to bfloat16 on the way count: a program that leaves them out, or rounds other values in their place, can miss the bound.
Values may be sent and summed in bfloat16 or wider, within the bound.
A program may use at most 128 MiB of HBM per device.

```python
import math
import jax
import jax.numpy as jnp
from jax import lax

D = 512
HEADS = 16
HEAD_DIM = 32
BLOCK = 128
NEIGH = 8
BLK_SLAB = 32
REACH = 16
BLOCKS = 128
ATOMS = 16384


def draw_atom_feats(key, part):
    key = jax.random.fold_in(key, 5)
    values = jnp.clip(jax.random.normal(key, (ATOMS, D), jnp.float32), -8.0, 8.0)
    return values.astype(jnp.bfloat16)


def draw_w_qkv(key, part):
    key = jax.random.fold_in(key, 7)
    first = jax.random.fold_in(key, 0)
    values = jnp.clip(jax.random.normal(first, (D, HEADS, 3 * HEAD_DIM), jnp.float32), -6.0, 6.0) / math.sqrt(D)
    return values.astype(jnp.bfloat16)


def draw_neighbours(key, part):
    key = jax.random.fold_in(key, 11)
    first, second = jax.random.split(key)
    candidates = jnp.concatenate([jnp.arange(-(REACH - 1), 0, dtype=jnp.int32), jnp.arange(1, REACH, dtype=jnp.int32)])
    block_keys = jax.random.split(first, BLOCKS)
    picks = jax.vmap(lambda one_key: jax.random.permutation(one_key, candidates))(block_keys)[:, :NEIGH - 2]
    block_ids = jnp.arange(BLOCKS, dtype=jnp.int32)
    side = jax.random.randint(second, (BLOCKS,), 0, 2, dtype=jnp.int32)
    edge = (REACH * (2 * side - 1)).astype(jnp.int32)
    offsets = jnp.concatenate([jnp.zeros((BLOCKS, 1), jnp.int32), picks, edge[:, None]], axis=1)
    return ((block_ids[:, None] + offsets) % BLOCKS).astype(jnp.int32)


def draw_counts(key, part):
    key = jax.random.fold_in(key, 13)
    first, second = jax.random.split(key)
    values = jax.random.randint(first, (BLOCKS,), BLOCK // 4, BLOCK + 1, dtype=jnp.int32)
    chosen = jax.random.randint(second, (BLOCKS // 4,), 0, 4, dtype=jnp.int32)
    block_ids = jnp.arange(BLOCKS, dtype=jnp.int32)
    within = block_ids % 4
    picked = chosen[block_ids // 4]
    values = jnp.where(within == picked, BLOCK, values)
    values = jnp.where(within == (picked + 2) % 4, BLOCK // 4, values)
    return values.astype(jnp.int32)


def block_scale(key, extent, cuts, least, top_value):
    gain = 1.0
    for axis_at, shards_of in cuts:
        heights = jax.random.uniform(jax.random.fold_in(jax.random.fold_in(key, 6), axis_at), (shards_of,), jnp.float32, least / len(cuts), top_value / len(cuts))
        gain = gain * jnp.repeat(jnp.exp(heights), extent[axis_at] // shards_of).reshape((-1,) + (1,) * (len(extent) - 1 - axis_at))
    return gain


def bell_draw(own_key, extent, spread, most, pieces=(), kind=jnp.bfloat16):
    gain = block_scale(own_key, extent, pieces, -0.22, 0.18) if pieces else 1.0
    result = jax.random.normal(own_key, extent, jnp.float32) * spread * gain
    return jnp.minimum(jnp.maximum(result, -most), most).astype(kind)


def setup_inputs(seed: int = 0, part: int = 0) -> dict:
    arg_keys = jax.random.split(jax.random.key(seed), 7)
    part_keys = jax.random.split(jax.random.fold_in(arg_keys[6], part), 7)
    atom_feats = draw_atom_feats(jax.random.fold_in(jax.random.fold_in(arg_keys[6], part), 71), part)
    w_qkv = draw_w_qkv(jax.random.fold_in(arg_keys[6], 71), part)
    w_out = bell_draw(arg_keys[2], (D, D), D ** -0.5, 0.25)
    neighbours = draw_neighbours(jax.random.fold_in(jax.random.fold_in(arg_keys[6], part), 71), part)
    counts = draw_counts(jax.random.fold_in(jax.random.fold_in(arg_keys[6], part), 71), part)
    d_out = bell_draw(part_keys[5], (ATOMS, D), 1.0, 6.0, ((0, 16),))
    return {"atom_feats": atom_feats, "w_qkv": w_qkv, "w_out": w_out, "neighbours": neighbours, "counts": counts, "d_out": d_out}


def reference(atom_feats, w_qkv, w_out, neighbours, counts, d_out):
    scale = 1.0 / math.sqrt(HEAD_DIM)
    flat_w = w_qkv.reshape(D, HEADS * 3 * HEAD_DIM)
    qkv_all = jnp.dot(atom_feats, flat_w, preferred_element_type=jnp.float32).astype(jnp.bfloat16)
    qkv_all = qkv_all.reshape(BLOCKS, BLOCK, HEADS, 3 * HEAD_DIM)
    queries = qkv_all[..., :HEAD_DIM]
    keyvals = qkv_all[..., HEAD_DIM:]
    slot_pos = jnp.arange(BLOCK, dtype=jnp.int32)
    row_valid = (slot_pos[None, :] < counts[:, None]).reshape(ATOMS, 1)
    group = min(BLK_SLAB, max(1, 512 // BLOCK))
    n_groups = BLOCKS // group
    query_groups = queries.reshape(n_groups, group, BLOCK, HEADS, HEAD_DIM)
    list_groups = neighbours.reshape(n_groups, group, NEIGH)

    def gather_keys(lists):
        picked = keyvals[lists].reshape(group, NEIGH * BLOCK, HEADS, 2 * HEAD_DIM)
        valid = (slot_pos[None, None, :] < counts[lists][..., None]).reshape(group, NEIGH * BLOCK)
        return (picked[..., :HEAD_DIM], picked[..., HEAD_DIM:], valid)

    def raw_scores(query_block, key_block, valid):
        scores = jnp.einsum('gqhd,gkhd->ghqk', query_block.astype(jnp.float32), key_block.astype(jnp.float32)) * scale
        return jnp.where(valid[:, None, None, :], scores, -jnp.inf)

    def forward_group(inputs):
        query_block, lists = inputs
        key_block, value_block, valid = gather_keys(lists)
        scores = raw_scores(query_block, key_block, valid)
        top = lax.optimization_barrier(jnp.max(scores, axis=-1, keepdims=True))
        log_total = top + jnp.log(lax.optimization_barrier(jnp.sum(jnp.exp(scores - top), axis=-1, keepdims=True)))
        probs = jnp.exp(scores - log_total).astype(jnp.bfloat16)
        attended = jnp.einsum('ghqk,gkhd->gqhd', probs.astype(jnp.float32), value_block.astype(jnp.float32))
        return (attended.astype(jnp.bfloat16), log_total)
    attended, log_totals = lax.map(forward_group, (query_groups, list_groups))
    attn_rows = attended.reshape(ATOMS, D)
    projected = jnp.dot(attn_rows, w_out, preferred_element_type=jnp.float32)
    layer_out = jnp.where(row_valid, projected, jnp.zeros_like(projected)).astype(jnp.bfloat16)
    masked_grad = jnp.where(row_valid, d_out, jnp.zeros_like(d_out))
    grad_wo = lax.dot_general(attn_rows, masked_grad, (((0,), (0,)), ((), ())), preferred_element_type=jnp.float32) / math.sqrt(ATOMS)
    d_attn = lax.dot_general(masked_grad, w_out, (((1,), (1,)), ((), ())), preferred_element_type=jnp.float32).astype(jnp.bfloat16)
    d_attn_groups = d_attn.reshape(n_groups, group, BLOCK, HEADS, HEAD_DIM)

    def backward_group(carry, inputs):
        query_block, lists, log_total, attended_block, grad_block = inputs
        key_block, value_block, valid = gather_keys(lists)
        scores = raw_scores(query_block, key_block, valid)
        weights = jnp.exp(scores - log_total)
        probs = weights.astype(jnp.bfloat16)
        delta = lax.optimization_barrier(jnp.sum(grad_block.astype(jnp.float32) * attended_block.astype(jnp.float32), axis=-1))
        delta = jnp.transpose(delta, (0, 2, 1))[..., None]
        grad_values = jnp.einsum('ghqk,gqhd->gkhd', probs.astype(jnp.float32), grad_block.astype(jnp.float32))
        grad_probs = jnp.einsum('gqhd,gkhd->ghqk', grad_block.astype(jnp.float32), value_block.astype(jnp.float32))
        grad_scores = (weights * (grad_probs - delta)).astype(jnp.bfloat16)
        grad_queries = jnp.einsum('ghqk,gkhd->gqhd', grad_scores.astype(jnp.float32), key_block.astype(jnp.float32)) * scale
        grad_keys = jnp.einsum('ghqk,gqhd->gkhd', grad_scores.astype(jnp.float32), query_block.astype(jnp.float32)) * scale
        both = jnp.concatenate([grad_keys, grad_values], axis=-1).reshape(group * NEIGH, BLOCK, HEADS, 2 * HEAD_DIM)
        carry = carry.at[lists.reshape(-1)].add(both)
        return (carry, grad_queries.astype(jnp.bfloat16))
    start_kv = jnp.zeros((BLOCKS, BLOCK, HEADS, 2 * HEAD_DIM), jnp.float32)
    grad_kv, grad_q = lax.scan(backward_group, start_kv, (query_groups, list_groups, log_totals, attended, d_attn_groups))
    grad_qkv = jnp.concatenate([grad_q.reshape(BLOCKS, BLOCK, HEADS, HEAD_DIM), grad_kv.astype(jnp.bfloat16)], axis=-1)
    grad_qkv = grad_qkv.reshape(ATOMS, HEADS * 3 * HEAD_DIM)
    grad_x = lax.dot_general(grad_qkv, flat_w, (((1,), (1,)), ((), ())), preferred_element_type=jnp.float32).astype(jnp.bfloat16)
    return (layer_out, grad_x, grad_wo)
```

```python
import functools
import math

import jax
import jax.numpy as jnp
from jax import lax
from jax.experimental import pallas as pl
from jax.experimental.pallas import tpu as pltpu
from jax.sharding import PartitionSpec as P

BLOCK = 128
NEIGH = 8
REACH = 16
VMEM_BYTES = 48 * 1024 * 1024


def from_behind(shard, axis, by):
    count = lax.axis_size(axis)
    return lax.ppermute(shard, axis, [(i, (i + by) % count) for i in range(count)])


def lookup_counts(block_ids, counts):
    table_ids = jnp.arange(counts.shape[0], dtype=jnp.int32)
    hits = block_ids[..., None] == table_ids
    return jnp.sum(jnp.where(hits, counts, 0), axis=-1)


def dot(a, b, dims):
    return lax.dot_general(a, b, (dims, ((), ())), preferred_element_type=jnp.float32)


def project_kernel(x_ref, g_ref, w_ref, wo_ref, out_ref):
    width = wo_ref.shape[0]
    qkv = dot(x_ref[...], w_ref[0], ((1,), (0,)))
    out_ref[0, :, : 3 * width] = qkv.astype(jnp.bfloat16)
    d_attn = dot(g_ref[...], wo_ref[...], ((1,), (1,)))
    out_ref[0, :, 3 * width :] = d_attn.astype(jnp.bfloat16)


def attention_kernel(
    heads, lists, list_counts, own_ref, kv_ref, att_ref, dq_ref, dkv_ref, s_ref, p_ref, g_ref
):
    step = pl.program_id(0)
    width = att_ref.shape[2]
    head_dim = width // heads
    lanes = heads * BLOCK
    scale = 1.0 / math.sqrt(head_dim)
    exp_scale = scale * math.log2(math.e)

    @pl.when(step == 0)
    def _():
        dkv_ref[...] = jnp.zeros_like(dkv_ref)

    row_head = lax.broadcasted_iota(jnp.int32, (width, lanes), 0) // head_dim
    lane_head = lax.broadcasted_iota(jnp.int32, (width, lanes), 1) // BLOCK
    diagonal = row_head == lane_head

    def spread(rows):
        turned = rows.astype(jnp.float32).T
        return jnp.where(diagonal, jnp.concatenate([turned] * heads, axis=1), 0.0)

    def gather_diagonal(full):
        parts = [
            full[h * head_dim : (h + 1) * head_dim, h * BLOCK : (h + 1) * BLOCK]
            for h in range(heads)
        ]
        return jnp.concatenate(parts, axis=0).T

    own = own_ref[0]
    q_bd = spread(own[:, :width]).astype(jnp.bfloat16)
    grad_bd = spread(own[:, 3 * width :])
    slots = lax.broadcasted_iota(jnp.int32, (BLOCK, 1), 0)
    ids = [lists[step * NEIGH + n] for n in range(NEIGH)]

    top = jnp.full((8, lanes), -jnp.inf, jnp.float32)
    for n in range(NEIGH):
        scores = dot(kv_ref[ids[n], :, :width], q_bd, ((1,), (0,)))
        scores = jnp.where(slots < list_counts[step * NEIGH + n], scores, -jnp.inf)
        s_ref[n] = scores
        top = jnp.maximum(top, jnp.max(scores.reshape(BLOCK // 8, 8, lanes), axis=0))
    top = jnp.max(top, axis=0, keepdims=True) * exp_scale

    total = jnp.zeros((8, lanes), jnp.float32)
    for n in range(NEIGH):
        p = jnp.exp2(s_ref[n] * exp_scale - top)
        total += jnp.sum(p.reshape(BLOCK // 8, 8, lanes), axis=0)
        p_ref[n * BLOCK : (n + 1) * BLOCK] = p.astype(jnp.bfloat16)
    inverse = 1.0 / jnp.sum(total, axis=0, keepdims=True)

    values = jnp.concatenate([kv_ref[ids[n], :, width:] for n in range(NEIGH)], axis=0)
    att_full = dot(values, p_ref[...], ((0,), (0,))) * inverse
    att_round = att_full.astype(jnp.bfloat16)
    att_ref[0] = gather_diagonal(att_full).astype(jnp.bfloat16)

    grad_bd = (grad_bd * inverse).astype(jnp.bfloat16)
    delta = jnp.sum(
        grad_bd.astype(jnp.float32) * att_round.astype(jnp.float32), axis=0, keepdims=True
    )
    for n in range(NEIGH):
        at = slice(n * BLOCK, (n + 1) * BLOCK)
        grad_probs = dot(kv_ref[ids[n], :, width:], grad_bd, ((1,), (0,)))
        p = p_ref[at]
        grad_scores = (p.astype(jnp.float32) * (grad_probs - delta)).astype(jnp.bfloat16)
        g_ref[at] = grad_scores
        dkv_ref[ids[n], :, :width] += dot(grad_scores, q_bd, ((1,), (1,))) * scale
        dkv_ref[ids[n], :, width:] += dot(p, grad_bd, ((1,), (1,)))

    keys = jnp.concatenate([kv_ref[ids[n], :, :width] for n in range(NEIGH)], axis=0)
    dq_full = dot(keys, g_ref[...], ((0,), (0,))) * scale
    dq_ref[0] = gather_diagonal(dq_full).astype(jnp.bfloat16)


def on_device(atom_feats, w_qkv, w_out, neighbours, counts, d_out):
    row_count, model_width = atom_feats.shape
    n_head = lax.axis_size("head")
    n_slab = lax.axis_size("slab")
    heads_all = w_qkv.shape[1]
    head_dim = w_qkv.shape[2] // 3
    own_heads = heads_all // n_head
    width = own_heads * head_dim
    slab_blocks = neighbours.shape[0]
    slab_rows = row_count * n_head
    total_blocks = slab_blocks * n_slab
    total_atoms = slab_rows * n_slab
    ext_blocks = slab_blocks + 2 * REACH
    head_index = lax.axis_index("head")
    slab_index = lax.axis_index("slab")
    bf16 = jnp.bfloat16

    row_global = (slab_index * n_head + head_index) * row_count + jnp.arange(
        row_count, dtype=jnp.int32
    )
    row_counts = lookup_counts(row_global // BLOCK, counts)
    row_valid = (row_global % BLOCK < row_counts)[:, None]
    masked_grad = jnp.where(row_valid, d_out, jnp.zeros_like(d_out))
    w_groups = jnp.transpose(
        w_qkv.reshape(model_width, n_head, own_heads, 3, head_dim), (1, 0, 3, 2, 4)
    ).reshape(n_head, model_width, 3 * width)

    projected = pl.pallas_call(
        project_kernel,
        grid=(n_head,),
        in_specs=[
            pl.BlockSpec((row_count, model_width), lambda g: (0, 0)),
            pl.BlockSpec((row_count, model_width), lambda g: (0, 0)),
            pl.BlockSpec((1, model_width, 3 * width), lambda g: (g, 0, 0)),
            pl.BlockSpec((width, model_width), lambda g: (g, 0)),
        ],
        out_specs=pl.BlockSpec((1, row_count, 4 * width), lambda g: (g, 0, 0)),
        out_shape=jax.ShapeDtypeStruct((n_head, row_count, 4 * width), bf16),
        compiler_params=pltpu.CompilerParams(vmem_limit_bytes=VMEM_BYTES),
    )(atom_feats, masked_grad, w_groups, w_out)
    own = lax.all_to_all(projected, "head", split_axis=0, concat_axis=0, tiled=True)
    own = own.reshape(slab_blocks, BLOCK, 4 * width)

    keyvals = own[:, :, width : 3 * width]
    before = from_behind(keyvals[slab_blocks - REACH :], "slab", 1)
    after = from_behind(keyvals[:REACH], "slab", -1)
    kv_ext = jnp.concatenate([before, keyvals, after], axis=0)
    local_lists = (neighbours - slab_index * slab_blocks + REACH) % total_blocks
    list_counts = lookup_counts(neighbours, counts)

    pairs = slab_rows * NEIGH * BLOCK * own_heads
    attended, grad_q, grad_kv = pl.pallas_call(
        functools.partial(attention_kernel, own_heads),
        grid_spec=pltpu.PrefetchScalarGridSpec(
            num_scalar_prefetch=2,
            grid=(slab_blocks,),
            in_specs=[
                pl.BlockSpec((1, BLOCK, 4 * width), lambda b, *_: (b, 0, 0)),
                pl.BlockSpec((ext_blocks, BLOCK, 2 * width), lambda b, *_: (0, 0, 0)),
            ],
            out_specs=[
                pl.BlockSpec((1, BLOCK, width), lambda b, *_: (b, 0, 0)),
                pl.BlockSpec((1, BLOCK, width), lambda b, *_: (b, 0, 0)),
                pl.BlockSpec((ext_blocks, BLOCK, 2 * width), lambda b, *_: (0, 0, 0)),
            ],
            scratch_shapes=[
                pltpu.VMEM((NEIGH, BLOCK, own_heads * BLOCK), jnp.float32),
                pltpu.VMEM((NEIGH * BLOCK, own_heads * BLOCK), bf16),
                pltpu.VMEM((NEIGH * BLOCK, own_heads * BLOCK), bf16),
            ],
        ),
        out_shape=[
            jax.ShapeDtypeStruct((slab_blocks, BLOCK, width), bf16),
            jax.ShapeDtypeStruct((slab_blocks, BLOCK, width), bf16),
            jax.ShapeDtypeStruct((ext_blocks, BLOCK, 2 * width), jnp.float32),
        ],
        compiler_params=pltpu.CompilerParams(vmem_limit_bytes=VMEM_BYTES),
        cost_estimate=pl.CostEstimate(
            flops=12 * pairs * head_dim, bytes_accessed=16 * 1024 * 1024, transcendentals=pairs
        ),
    )(local_lists.reshape(-1), list_counts.reshape(-1), own, kv_ext)

    from_next = from_behind(grad_kv[:REACH].astype(bf16), "slab", -1).astype(jnp.float32)
    from_prev = from_behind(grad_kv[REACH + slab_blocks :].astype(bf16), "slab", 1).astype(
        jnp.float32
    )
    att_dq = jnp.concatenate(
        [attended.reshape(n_head, row_count, width), grad_q.reshape(n_head, row_count, width)],
        axis=2,
    )
    att_dq = lax.all_to_all(att_dq, "head", split_axis=0, concat_axis=0, tiled=True)
    attn_rows = jnp.transpose(att_dq[:, :, :width], (1, 0, 2)).reshape(row_count, model_width)

    layer_out = jnp.dot(attn_rows, w_out, preferred_element_type=jnp.float32)
    layer_out = jnp.where(row_valid, layer_out, jnp.zeros_like(layer_out)).astype(bf16)
    term = dot(attn_rows, masked_grad, ((0,), (0,))) / math.sqrt(total_atoms)
    term = term.astype(bf16).reshape(n_head, model_width // n_head, n_slab, model_width // n_slab)
    term = jnp.transpose(term, (2, 0, 1, 3)).reshape(
        n_slab * n_head, model_width // n_head, model_width // n_slab
    )
    term = lax.all_to_all(term, ("slab", "head"), split_axis=0, concat_axis=0, tiled=True)
    grad_wo = jnp.sum(term.astype(jnp.float32), axis=0)

    own_grad = grad_kv[REACH : REACH + slab_blocks]
    own_grad = own_grad.at[slab_blocks - REACH :].add(from_next)
    own_grad = own_grad.at[:REACH].add(from_prev)
    own_grad = own_grad.astype(bf16).reshape(n_head, row_count, 2 * width)
    grad_kv_rows = lax.all_to_all(own_grad, "head", split_axis=0, concat_axis=0, tiled=True)
    grad_x = jnp.einsum(
        "grc,gmc->rm", att_dq[:, :, width:], w_groups[:, :, :width],
        preferred_element_type=jnp.float32,
    ) + jnp.einsum(
        "grc,gmc->rm", grad_kv_rows, w_groups[:, :, width:], preferred_element_type=jnp.float32
    )
    return (layer_out, grad_x.astype(bf16), grad_wo)


def solution(mesh):
    placed = (
        P(("rep", "slab", "head"), None),
        P(),
        P(),
        P(("rep", "slab"), None),
        P("rep"),
        P(("rep", "slab", "head"), None),
    )
    return jax.shard_map(
        on_device,
        mesh=mesh,
        in_specs=placed,
        out_specs=(
            P(("rep", "slab", "head"), None),
            P(("rep", "slab", "head"), None),
            P(("rep", "head"), "slab"),
        ),
        check_vma=False,
    )
```

```python
import functools
import math

import jax
import jax.numpy as jnp
from jax import lax
from jax.experimental import pallas as pl
from jax.experimental.pallas import tpu as pltpu
from jax.sharding import PartitionSpec as P

BLOCK = 128
NEIGH = 8
REACH = 16
TOGETHER = 2
VMEM_BYTES = 48 * 1024 * 1024


def from_behind(shard, axis, by):
    count = lax.axis_size(axis)
    return lax.ppermute(shard, axis, [(i, (i + by) % count) for i in range(count)])


def lookup_counts(block_ids, counts):
    table_ids = jnp.arange(counts.shape[0], dtype=jnp.int32)
    hits = block_ids[..., None] == table_ids
    return jnp.sum(jnp.where(hits, counts, 0), axis=-1)


def dot(a, b, dims):
    return lax.dot_general(a, b, (dims, ((), ())), preferred_element_type=jnp.float32)


def project_kernel(parts, x_ref, g_ref, w_ref, wo_ref, *out_refs):
    width = wo_ref.shape[0] // parts
    qkv = dot(x_ref[...], w_ref[0], ((1,), (0,))).astype(jnp.bfloat16)
    d_attn = dot(g_ref[...], wo_ref[...], ((1,), (1,))).astype(jnp.bfloat16)
    for part, out_ref in enumerate(out_refs):
        columns = slice(part * width, (part + 1) * width)
        wide = slice(part * 3 * width, (part + 1) * 3 * width)
        out_ref[0] = jnp.concatenate([qkv[:, wide], d_attn[:, columns]], axis=1)


def attention_kernel(
    heads, lists, list_counts, own_ref, kv_ref, out_ref, dkv_ref,
    turned_ref, l_ref, lt_ref, s_ref, p_ref, g_ref, sum_ref,
):
    step = pl.program_id(0)
    together = own_ref.shape[0]
    ext_blocks = kv_ref.shape[0]
    width = out_ref.shape[2] // 2
    head_dim = width // heads
    lanes = heads * BLOCK
    scale = 1.0 / math.sqrt(head_dim)
    exp_scale = scale * math.log2(math.e)
    each = range(together)
    bf16 = jnp.bfloat16

    @pl.when(step == 0)
    def _():
        dkv_ref[...] = jnp.zeros_like(dkv_ref)

        @pl.loop(0, ext_blocks)
        def _(block):
            turned_ref[block] = kv_ref[block].T

    row_head = lax.broadcasted_iota(jnp.int32, (2 * width, lanes), 0) // head_dim
    lane_head = lax.broadcasted_iota(jnp.int32, (2 * width, lanes), 1) // BLOCK
    column = lax.broadcasted_iota(jnp.int32, (1, 2 * width), 1)
    column_scale = jnp.where(column < width, scale, 1.0)
    slots = lax.broadcasted_iota(jnp.int32, (BLOCK, 1), 0)
    first = step * (together * NEIGH)
    ids = [[lists[first + u * NEIGH + n] for n in range(NEIGH)] for u in each]
    spans = [slice(n * BLOCK, (n + 1) * BLOCK) for n in range(NEIGH)]

    def valid(u, n):
        return slots < list_counts[first + u * NEIGH + n]

    def pick_diagonal(full):
        return [
            full[h * head_dim : (h + 1) * head_dim, h * BLOCK : (h + 1) * BLOCK]
            for h in range(heads)
        ]

    q_bd, grad_bd = [], []
    for u in each:
        for n in range(NEIGH):
            l_ref[u, spans[n]] = kv_ref[ids[u][n]]
            lt_ref[u, :, spans[n]] = turned_ref[ids[u][n]]
        turned = own_ref[u, :, 2 * width :].astype(jnp.float32).T
        turned = jnp.concatenate([turned] * heads, axis=1)
        q_bd.append(jnp.where(row_head == lane_head, turned, 0.0).astype(bf16))
        grad_bd.append(jnp.where(row_head - heads == lane_head, turned, 0.0))
    for u in each:
        s_ref[u] = dot(l_ref[u], q_bd[u], ((1,), (0,)))

    inverse = []
    for u in each:
        top = jnp.full((8, lanes), -jnp.inf, jnp.float32)
        for n in range(NEIGH):
            scores = jnp.where(valid(u, n), s_ref[u, spans[n]], -jnp.inf)
            top = jnp.maximum(top, jnp.max(scores.reshape(BLOCK // 8, 8, lanes), axis=0))
        top = jnp.max(top, axis=0, keepdims=True) * exp_scale
        total = jnp.zeros((8, lanes), jnp.float32)
        for n in range(NEIGH):
            p = jnp.where(valid(u, n), jnp.exp2(s_ref[u, spans[n]] * exp_scale - top), 0.0)
            total += jnp.sum(p.reshape(BLOCK // 8, 8, lanes), axis=0)
            p_ref[u, spans[n]] = p.astype(bf16)
        inverse.append(1.0 / jnp.sum(total, axis=0, keepdims=True))

    delta, attended, right = [], [], []
    for u in each:
        att_full = dot(lt_ref[u, width:], p_ref[u], ((1,), (0,))) * inverse[u]
        attended.append(att_full)
        att_round = att_full.astype(bf16).astype(jnp.float32)
        rounded = (grad_bd[u] * inverse[u]).astype(bf16)
        grad_bd[u] = rounded
        delta.append(
            jnp.sum(rounded[width:].astype(jnp.float32) * att_round, axis=0, keepdims=True)
        )
        right.append(jnp.concatenate([q_bd[u].T, rounded.T], axis=0))
    for u in each:
        s_ref[u] = dot(l_ref[u], grad_bd[u], ((1,), (0,)))
    for u in each:
        for n in range(NEIGH):
            p = p_ref[u, spans[n]].astype(jnp.float32)
            g_ref[u, spans[n]] = (p * (s_ref[u, spans[n]] - delta[u])).astype(bf16)
    for u in each:
        both = jnp.concatenate([g_ref[u], p_ref[u]], axis=1)
        sum_ref[u] = dot(both, right[u], ((1,), (0,))) * column_scale
    for u in each:
        dq_full = dot(lt_ref[u, :width], g_ref[u], ((1,), (0,))) * scale
        rows = pick_diagonal(attended[u]) + pick_diagonal(dq_full)
        out_ref[u] = jnp.concatenate(rows, axis=0).T.astype(bf16)
    for u in each:
        for n in range(NEIGH):
            dkv_ref[ids[u][n]] += sum_ref[u, spans[n]]


def exchange(blocks):
    return lax.all_to_all(blocks, "head", split_axis=0, concat_axis=0, tiled=True)


def after_of(value, earlier):
    return lax.optimization_barrier((value, earlier))[0]


def on_device(atom_feats, w_qkv, w_out, neighbours, counts, d_out):
    row_count, model_width = atom_feats.shape
    n_head = lax.axis_size("head")
    n_slab = lax.axis_size("slab")
    heads_all = w_qkv.shape[1]
    head_dim = w_qkv.shape[2] // 3
    own_heads = heads_all // n_head
    slab_blocks = neighbours.shape[0]
    slab_rows = row_count * n_head
    total_blocks = slab_blocks * n_slab
    total_atoms = slab_rows * n_slab
    ext_blocks = slab_blocks + 2 * REACH
    list_rows = NEIGH * BLOCK
    head_index = lax.axis_index("head")
    slab_index = lax.axis_index("slab")
    bf16 = jnp.bfloat16

    row_global = (slab_index * n_head + head_index) * row_count + jnp.arange(
        row_count, dtype=jnp.int32
    )
    row_counts = lookup_counts(row_global // BLOCK, counts)
    row_valid = (row_global % BLOCK < row_counts)[:, None]
    masked_grad = jnp.where(row_valid, d_out, jnp.zeros_like(d_out))
    parts = 2 if own_heads % 2 == 0 else 1
    heads = own_heads // parts
    width = heads * head_dim
    w_groups = w_qkv.reshape(model_width, n_head, parts, heads, 3, head_dim)
    w_groups = jnp.transpose(
        jnp.stack([w_groups[..., t, :] for t in (1, 2, 0)], axis=4), (1, 0, 2, 4, 3, 5)
    ).reshape(n_head, model_width, parts * 3 * width)

    projected = pl.pallas_call(
        functools.partial(project_kernel, parts),
        grid=(n_head,),
        in_specs=[
            pl.BlockSpec((row_count, model_width), lambda g: (0, 0)),
            pl.BlockSpec((row_count, model_width), lambda g: (0, 0)),
            pl.BlockSpec((1, model_width, parts * 3 * width), lambda g: (g, 0, 0)),
            pl.BlockSpec((parts * width, model_width), lambda g: (g, 0)),
        ],
        out_specs=[pl.BlockSpec((1, row_count, 4 * width), lambda g: (g, 0, 0))] * parts,
        out_shape=[jax.ShapeDtypeStruct((n_head, row_count, 4 * width), bf16)] * parts,
        compiler_params=pltpu.CompilerParams(vmem_limit_bytes=VMEM_BYTES),
    )(atom_feats, masked_grad, w_groups, w_out)
    local_lists = (neighbours - slab_index * slab_blocks + REACH) % total_blocks
    local_lists = local_lists.reshape(-1)
    list_counts = lookup_counts(neighbours, counts).reshape(-1)
    pairs = slab_rows * NEIGH * BLOCK * heads

    def attend(own, before, after):
        kv_ext = jnp.concatenate([before, own[:, :, : 2 * width], after], axis=0)
        return pl.pallas_call(
            functools.partial(attention_kernel, heads),
            grid_spec=pltpu.PrefetchScalarGridSpec(
                num_scalar_prefetch=2,
                grid=(slab_blocks // TOGETHER,),
                in_specs=[
                    pl.BlockSpec((TOGETHER, BLOCK, 4 * width), lambda b, *_: (b, 0, 0)),
                    pl.BlockSpec((ext_blocks, BLOCK, 2 * width), lambda b, *_: (0, 0, 0)),
                ],
                out_specs=[
                    pl.BlockSpec((TOGETHER, BLOCK, 2 * width), lambda b, *_: (b, 0, 0)),
                    pl.BlockSpec((ext_blocks, BLOCK, 2 * width), lambda b, *_: (0, 0, 0)),
                ],
                scratch_shapes=[
                    pltpu.VMEM((ext_blocks, 2 * width, BLOCK), bf16),
                    pltpu.VMEM((TOGETHER, list_rows, 2 * width), bf16),
                    pltpu.VMEM((TOGETHER, 2 * width, list_rows), bf16),
                    pltpu.VMEM((TOGETHER, list_rows, heads * BLOCK), jnp.float32),
                    pltpu.VMEM((TOGETHER, list_rows, heads * BLOCK), bf16),
                    pltpu.VMEM((TOGETHER, list_rows, heads * BLOCK), bf16),
                    pltpu.VMEM((TOGETHER, list_rows, 2 * width), jnp.float32),
                ],
            ),
            out_shape=[
                jax.ShapeDtypeStruct((slab_blocks, BLOCK, 2 * width), bf16),
                jax.ShapeDtypeStruct((ext_blocks, BLOCK, 2 * width), jnp.float32),
            ],
            compiler_params=pltpu.CompilerParams(vmem_limit_bytes=VMEM_BYTES),
            cost_estimate=pl.CostEstimate(
                flops=400 * pairs * head_dim, bytes_accessed=8 << 20, transcendentals=pairs
            ),
        )(local_lists, list_counts, own, kv_ext)

    received, results = [], []
    for part in range(parts):
        blocks = projected[part]
        if part:
            blocks = after_of(blocks, received[-1])
        received.append(exchange(blocks).reshape(slab_blocks, BLOCK, 4 * width))
    for part in range(parts):
        own = received[part]
        keyvals = own[:, :, : 2 * width]
        before = from_behind(keyvals[slab_blocks - REACH :], "slab", 1)
        after = from_behind(keyvals[:REACH], "slab", -1)
        results.append(attend(own, before, after))

    att_dq, grad_kv_rows = [], []
    for rows, grad_kv in results:
        from_next = from_behind(grad_kv[:REACH].astype(bf16), "slab", -1)
        from_prev = from_behind(grad_kv[REACH + slab_blocks :].astype(bf16), "slab", 1)
        att_dq.append(exchange(rows.reshape(n_head, row_count, 2 * width)))
        own_grad = grad_kv[REACH : REACH + slab_blocks]
        own_grad = own_grad.at[slab_blocks - REACH :].add(from_next.astype(jnp.float32))
        own_grad = own_grad.at[:REACH].add(from_prev.astype(jnp.float32))
        own_grad = own_grad.astype(bf16).reshape(n_head, row_count, 2 * width)
        grad_kv_rows.append(exchange(own_grad))

    attn_rows = jnp.stack([rows[:, :, :width] for rows in att_dq], axis=1)
    attn_rows = jnp.transpose(attn_rows, (2, 0, 1, 3)).reshape(row_count, model_width)
    layer_out = jnp.dot(attn_rows, w_out, preferred_element_type=jnp.float32)
    layer_out = jnp.where(row_valid, layer_out, jnp.zeros_like(layer_out)).astype(bf16)
    term = dot(attn_rows, masked_grad, ((0,), (0,))) / math.sqrt(total_atoms)
    term = term.astype(bf16).reshape(n_head, model_width // n_head, n_slab, model_width // n_slab)
    term = jnp.transpose(term, (2, 0, 1, 3)).reshape(
        n_slab * n_head, model_width // n_head, model_width // n_slab
    )
    term = lax.all_to_all(term, ("slab", "head"), split_axis=0, concat_axis=0, tiled=True)
    grad_wo = jnp.sum(term.astype(jnp.float32), axis=0)

    grad_x = jnp.zeros((row_count, model_width), jnp.float32)
    for part in range(parts):
        columns = [grad_kv_rows[part], att_dq[part][:, :, width:]]
        columns = jnp.concatenate(columns, axis=2)
        weights = w_groups[:, :, part * 3 * width : (part + 1) * 3 * width]
        grad_x += jnp.einsum("grc,gmc->rm", columns, weights, preferred_element_type=jnp.float32)
    return (layer_out, grad_x.astype(bf16), grad_wo)


def solution(mesh):
    placed = (
        P(("rep", "slab", "head"), None),
        P(),
        P(),
        P(("rep", "slab"), None),
        P("rep"),
        P(("rep", "slab", "head"), None),
    )
    return jax.shard_map(
        on_device,
        mesh=mesh,
        in_specs=placed,
        out_specs=(
            P(("rep", "slab", "head"), None),
            P(("rep", "slab", "head"), None),
            P(("rep", "head"), "slab"),
        ),
        check_vma=False,
    )
```

```python
import functools
import math

import jax
import jax.numpy as jnp
from jax import lax
from jax.experimental import pallas as pl
from jax.experimental.pallas import tpu as pltpu
from jax.sharding import PartitionSpec as P

BLOCK = 128
NEIGH = 8
REACH = 16
TOGETHER = 4
VMEM_BYTES = 48 * 1024 * 1024


def from_behind(shard, axis, by):
    count = lax.axis_size(axis)
    return lax.ppermute(shard, axis, [(i, (i + by) % count) for i in range(count)])


def lookup_counts(block_ids, counts):
    table_ids = jnp.arange(counts.shape[0], dtype=jnp.int32)
    hits = block_ids[..., None] == table_ids
    return jnp.sum(jnp.where(hits, counts, 0), axis=-1)


def dot(a, b, dims):
    return lax.dot_general(a, b, (dims, ((), ())), preferred_element_type=jnp.float32)


def project_kernel(parts, x_ref, g_ref, w_ref, wo_ref, *out_refs):
    width = wo_ref.shape[0] // parts
    qkv = dot(x_ref[...], w_ref[0], ((1,), (0,))).astype(jnp.bfloat16)
    d_attn = dot(g_ref[...], wo_ref[...], ((1,), (1,))).astype(jnp.bfloat16)
    for part, out_ref in enumerate(out_refs):
        columns = slice(part * width, (part + 1) * width)
        wide = slice(part * 3 * width, (part + 1) * 3 * width)
        out_ref[0] = jnp.concatenate([qkv[:, wide], d_attn[:, columns]], axis=1)


def attention_kernel(
    heads, lists, list_counts, own_ref, kv_ref, out_ref, low_ref, dkv_ref, high_ref,
    acc_ref, turned_ref, l_ref, lt_ref, s_ref, p_ref, g_ref, sum_ref,
):
    step = pl.program_id(0)
    together = own_ref.shape[0]
    ext_blocks = kv_ref.shape[0]
    width = out_ref.shape[2] // 2
    own_blocks = dkv_ref.shape[0]
    head_dim = width // heads
    lanes = heads * BLOCK
    scale = 1.0 / math.sqrt(head_dim)
    exp_scale = scale * math.log2(math.e)
    each = range(together)
    bf16 = jnp.bfloat16

    @pl.when(step == 0)
    def _():
        acc_ref[...] = jnp.zeros_like(acc_ref)

        @pl.loop(0, ext_blocks)
        def _(block):
            turned_ref[block] = kv_ref[block].T

    row_head = lax.broadcasted_iota(jnp.int32, (2 * width, lanes), 0) // head_dim
    lane_head = lax.broadcasted_iota(jnp.int32, (2 * width, lanes), 1) // BLOCK
    column = lax.broadcasted_iota(jnp.int32, (1, 2 * width), 1)
    column_scale = jnp.where(column < width, scale, 1.0)
    slots = lax.broadcasted_iota(jnp.int32, (BLOCK, 1), 0)
    first = step * (together * NEIGH)
    ids = [[lists[first + u * NEIGH + n] for n in range(NEIGH)] for u in each]
    spans = [slice(n * BLOCK, (n + 1) * BLOCK) for n in range(NEIGH)]

    def valid(u, n):
        return slots < list_counts[first + u * NEIGH + n]

    def pick_diagonal(full):
        return [
            full[h * head_dim : (h + 1) * head_dim, h * BLOCK : (h + 1) * BLOCK]
            for h in range(heads)
        ]

    q_bd, grad_bd = [], []
    for u in each:
        for n in range(NEIGH):
            l_ref[u, spans[n]] = kv_ref[ids[u][n]]
            lt_ref[u, :, spans[n]] = turned_ref[ids[u][n]]
        turned = own_ref[u, :, 2 * width :].astype(jnp.float32).T
        turned = jnp.concatenate([turned] * heads, axis=1)
        q_bd.append(jnp.where(row_head == lane_head, turned, 0.0).astype(bf16))
        grad_bd.append(jnp.where(row_head - heads == lane_head, turned, 0.0))
    for u in each:
        s_ref[u] = dot(l_ref[u], q_bd[u], ((1,), (0,)))

    inverse = []
    for u in each:
        top = jnp.full((8, lanes), -jnp.inf, jnp.float32)
        for n in range(NEIGH):
            scores = jnp.where(valid(u, n), s_ref[u, spans[n]], -jnp.inf)
            top = jnp.maximum(top, jnp.max(scores.reshape(BLOCK // 8, 8, lanes), axis=0))
        top = jnp.max(top, axis=0, keepdims=True) * exp_scale
        total = jnp.zeros((8, lanes), jnp.float32)
        for n in range(NEIGH):
            p = jnp.where(valid(u, n), jnp.exp2(s_ref[u, spans[n]] * exp_scale - top), 0.0)
            total += jnp.sum(p.reshape(BLOCK // 8, 8, lanes), axis=0)
            p_ref[u, spans[n]] = p.astype(bf16)
        inverse.append(1.0 / jnp.sum(total, axis=0, keepdims=True))

    delta, attended, right = [], [], []
    for u in each:
        att_full = dot(lt_ref[u, width:], p_ref[u], ((1,), (0,))) * inverse[u]
        attended.append(att_full)
        att_round = att_full.astype(bf16).astype(jnp.float32)
        rounded = (grad_bd[u] * inverse[u]).astype(bf16)
        grad_bd[u] = rounded
        delta.append(
            jnp.sum(rounded[width:].astype(jnp.float32) * att_round, axis=0, keepdims=True)
        )
        right.append(jnp.concatenate([q_bd[u].T, rounded.T], axis=0))
    for u in each:
        s_ref[u] = dot(l_ref[u], grad_bd[u], ((1,), (0,)))
    for u in each:
        for n in range(NEIGH):
            p = p_ref[u, spans[n]].astype(jnp.float32)
            g_ref[u, spans[n]] = (p * (s_ref[u, spans[n]] - delta[u])).astype(bf16)
    for u in each:
        both = jnp.concatenate([g_ref[u], p_ref[u]], axis=1)
        sum_ref[u] = dot(both, right[u], ((1,), (0,))) * column_scale
    for u in each:
        dq_full = dot(lt_ref[u, :width], g_ref[u], ((1,), (0,))) * scale
        rows = pick_diagonal(attended[u]) + pick_diagonal(dq_full)
        out_ref[u] = jnp.concatenate(rows, axis=0).T.astype(bf16)
    for u in each:
        for n in range(NEIGH):
            acc_ref[ids[u][n]] += sum_ref[u, spans[n]]

    @pl.when(step == pl.num_programs(0) - 1)
    def _():
        low_ref[...] = acc_ref[:REACH].astype(bf16)
        dkv_ref[...] = acc_ref[REACH : REACH + own_blocks]
        high_ref[...] = acc_ref[REACH + own_blocks :].astype(bf16)


def exchange(blocks):
    return lax.all_to_all(blocks, "head", split_axis=0, concat_axis=0, tiled=True)


def after_of(value, earlier):
    return lax.optimization_barrier((value, earlier))[0]


def on_device(atom_feats, w_qkv, w_out, neighbours, counts, d_out):
    row_count, model_width = atom_feats.shape
    n_head = lax.axis_size("head")
    n_slab = lax.axis_size("slab")
    heads_all = w_qkv.shape[1]
    head_dim = w_qkv.shape[2] // 3
    own_heads = heads_all // n_head
    slab_blocks = neighbours.shape[0]
    slab_rows = row_count * n_head
    total_blocks = slab_blocks * n_slab
    total_atoms = slab_rows * n_slab
    ext_blocks = slab_blocks + 2 * REACH
    list_rows = NEIGH * BLOCK
    head_index = lax.axis_index("head")
    slab_index = lax.axis_index("slab")
    bf16 = jnp.bfloat16

    row_global = (slab_index * n_head + head_index) * row_count + jnp.arange(
        row_count, dtype=jnp.int32
    )
    row_counts = lookup_counts(row_global // BLOCK, counts)
    row_valid = (row_global % BLOCK < row_counts)[:, None]
    masked_grad = jnp.where(row_valid, d_out, jnp.zeros_like(d_out))
    parts = 2 if own_heads % 2 == 0 else 1
    heads = own_heads // parts
    width = heads * head_dim
    w_groups = w_qkv.reshape(model_width, n_head, parts, heads, 3, head_dim)
    w_groups = jnp.transpose(
        jnp.stack([w_groups[..., t, :] for t in (1, 2, 0)], axis=4), (1, 0, 2, 4, 3, 5)
    ).reshape(n_head, model_width, parts * 3 * width)

    projected = pl.pallas_call(
        functools.partial(project_kernel, parts),
        grid=(n_head,),
        in_specs=[
            pl.BlockSpec((row_count, model_width), lambda g: (0, 0)),
            pl.BlockSpec((row_count, model_width), lambda g: (0, 0)),
            pl.BlockSpec((1, model_width, parts * 3 * width), lambda g: (g, 0, 0)),
            pl.BlockSpec((parts * width, model_width), lambda g: (g, 0)),
        ],
        out_specs=[pl.BlockSpec((1, row_count, 4 * width), lambda g: (g, 0, 0))] * parts,
        out_shape=[jax.ShapeDtypeStruct((n_head, row_count, 4 * width), bf16)] * parts,
        compiler_params=pltpu.CompilerParams(vmem_limit_bytes=VMEM_BYTES),
    )(atom_feats, masked_grad, w_groups, w_out)
    local_lists = (neighbours - slab_index * slab_blocks + REACH) % total_blocks
    local_lists = local_lists.reshape(-1)
    list_counts = lookup_counts(neighbours, counts).reshape(-1)
    pairs = slab_rows * NEIGH * BLOCK * heads

    def attend(own, before, after):
        kv_ext = jnp.concatenate([before, own[:, :, : 2 * width], after], axis=0)
        return pl.pallas_call(
            functools.partial(attention_kernel, heads),
            grid_spec=pltpu.PrefetchScalarGridSpec(
                num_scalar_prefetch=2,
                grid=(slab_blocks // TOGETHER,),
                in_specs=[
                    pl.BlockSpec((TOGETHER, BLOCK, 4 * width), lambda b, *_: (b, 0, 0)),
                    pl.BlockSpec((ext_blocks, BLOCK, 2 * width), lambda b, *_: (0, 0, 0)),
                ],
                out_specs=[
                    pl.BlockSpec((TOGETHER, BLOCK, 2 * width), lambda b, *_: (b, 0, 0)),
                    pl.BlockSpec((REACH, BLOCK, 2 * width), lambda b, *_: (0, 0, 0)),
                    pl.BlockSpec((slab_blocks, BLOCK, 2 * width), lambda b, *_: (0, 0, 0)),
                    pl.BlockSpec((REACH, BLOCK, 2 * width), lambda b, *_: (0, 0, 0)),
                ],
                scratch_shapes=[
                    pltpu.VMEM((ext_blocks, BLOCK, 2 * width), jnp.float32),
                    pltpu.VMEM((ext_blocks, 2 * width, BLOCK), bf16),
                    pltpu.VMEM((TOGETHER, list_rows, 2 * width), bf16),
                    pltpu.VMEM((TOGETHER, 2 * width, list_rows), bf16),
                    pltpu.VMEM((TOGETHER, list_rows, heads * BLOCK), jnp.float32),
                    pltpu.VMEM((TOGETHER, list_rows, heads * BLOCK), bf16),
                    pltpu.VMEM((TOGETHER, list_rows, heads * BLOCK), bf16),
                    pltpu.VMEM((TOGETHER, list_rows, 2 * width), jnp.float32),
                ],
            ),
            out_shape=[
                jax.ShapeDtypeStruct((slab_blocks, BLOCK, 2 * width), bf16),
                jax.ShapeDtypeStruct((REACH, BLOCK, 2 * width), bf16),
                jax.ShapeDtypeStruct((slab_blocks, BLOCK, 2 * width), jnp.float32),
                jax.ShapeDtypeStruct((REACH, BLOCK, 2 * width), bf16),
            ],
            compiler_params=pltpu.CompilerParams(vmem_limit_bytes=VMEM_BYTES),
            cost_estimate=pl.CostEstimate(
                flops=400 * pairs * head_dim, bytes_accessed=8 << 20, transcendentals=pairs
            ),
        )(local_lists, list_counts, own, kv_ext)

    received, results = [], []
    for part in range(parts):
        blocks = projected[part]
        if part:
            blocks = after_of(blocks, received[-1])
        received.append(exchange(blocks).reshape(slab_blocks, BLOCK, 4 * width))
    for part in range(parts):
        own = received[part]
        keyvals = own[:, :, : 2 * width]
        before = from_behind(keyvals[slab_blocks - REACH :], "slab", 1)
        after = from_behind(keyvals[:REACH], "slab", -1)
        results.append(attend(own, before, after))

    att_dq, grad_kv_rows = [], []
    for rows, low, own_grad, high in results:
        from_next = from_behind(low, "slab", -1)
        from_prev = from_behind(high, "slab", 1)
        att_dq.append(exchange(rows.reshape(n_head, row_count, 2 * width)))
        own_grad = own_grad.at[slab_blocks - REACH :].add(from_next.astype(jnp.float32))
        own_grad = own_grad.at[:REACH].add(from_prev.astype(jnp.float32))
        own_grad = own_grad.astype(bf16).reshape(n_head, row_count, 2 * width)
        grad_kv_rows.append(exchange(own_grad))

    attn_rows = jnp.stack([rows[:, :, :width] for rows in att_dq], axis=1)
    attn_rows = jnp.transpose(attn_rows, (2, 0, 1, 3)).reshape(row_count, model_width)
    layer_out = jnp.dot(attn_rows, w_out, preferred_element_type=jnp.float32)
    layer_out = jnp.where(row_valid, layer_out, jnp.zeros_like(layer_out)).astype(bf16)
    term = dot(attn_rows, masked_grad, ((0,), (0,))) / math.sqrt(total_atoms)
    term = term.astype(bf16).reshape(n_head, model_width // n_head, n_slab, model_width // n_slab)
    term = jnp.transpose(term, (2, 0, 1, 3)).reshape(
        n_slab * n_head, model_width // n_head, model_width // n_slab
    )
    term = lax.all_to_all(term, ("slab", "head"), split_axis=0, concat_axis=0, tiled=True)
    grad_wo = jnp.sum(term.astype(jnp.float32), axis=0)

    grad_x = jnp.zeros((row_count, model_width), jnp.float32)
    for part in range(parts):
        columns = [grad_kv_rows[part], att_dq[part][:, :, width:]]
        columns = jnp.concatenate(columns, axis=2)
        weights = w_groups[:, :, part * 3 * width : (part + 1) * 3 * width]
        grad_x += jnp.einsum("grc,gmc->rm", columns, weights, preferred_element_type=jnp.float32)
    return (layer_out, grad_x.astype(bf16), grad_wo)


def solution(mesh):
    placed = (
        P(("rep", "slab", "head"), None),
        P(),
        P(),
        P(("rep", "slab"), None),
        P("rep"),
        P(("rep", "slab", "head"), None),
    )
    return jax.shard_map(
        on_device,
        mesh=mesh,
        in_specs=placed,
        out_specs=(
            P(("rep", "slab", "head"), None),
            P(("rep", "slab", "head"), None),
            P(("rep", "head"), "slab"),
        ),
        check_vma=False,
    )
```
